32 devices in a mesh: dp: 2 (over x), expert: 16 (over z, y, core).
Axes of the slice: x: 2, y: 2, z: 4, core: 2. Of those that a mesh axis runs over, the one named last changes fastest.
Arguments:
- tokens: bfloat16 [4096, 1024], P(('dp', 'expert')), may hold values from -6 to 6
- cotangent: bfloat16 [4096, 1024], P(('dp', 'expert')), may hold values from -6 to 6
- pick_lists: int32 [2, 16, 128], P('dp'), may hold values from 0 to 2047, as said below
- combine: float32 [2, 16, 128], P('dp'), may hold values from 0.1 to 1
- w_gate: bfloat16 [16, 1024, 1024], P('expert', 'dp'), may hold values from -0.1875 to 0.1875
- w_up: bfloat16 [16, 1024, 1024], P('expert', 'dp'), may hold values from -0.1875 to 0.1875
- w_down: bfloat16 [16, 1024, 1024], P('expert', 'dp'), may hold values from -0.1875 to 0.1875
Outputs:
- layer_out: bfloat16 [4096, 1024], P(('dp', 'expert'))
- tokens_grad: bfloat16 [4096, 1024], P(('dp', 'expert'))
- grad_gate: bfloat16 [16, 1024, 1024], P('expert', 'dp')
- grad_up: bfloat16 [16, 1024, 1024], P('expert', 'dp')
- grad_down: bfloat16 [16, 1024, 1024], P('expert', 'dp')
The draws below stay inside these ranges and needn't reach their ends.
Inputs may be any that keep to these rules, and one draw needn't show every extreme that they name: Each list pick_lists[r, e] names 128 distinct tokens of replica r. Token numbers j * 128 to (j + 1) * 128 - 1 are those of the device with index j on the expert axis; at most 16 picks of one expert in one replica fall among one device's tokens, and for every expert and replica exactly 16 fall among some device's.
All inputs are finite; a program needn't handle non-finite values.
Results may differ from the reference program's by a relative error of at most 0.013.
Values may be sent and summed in bfloat16 or wider, within the bound.
A program may use at most 64 MiB of HBM per device.

```python
import jax
import jax.numpy as jnp
from jax import lax

D = 1024
FF = 1024
TOK_DEV = 128
EXPERTS = 16
CAP = 128
SLOT = 16
TOKENS_REP = 2048
TOKENS = 4096
N_DP = 2
N_EXPERT = 16


def draw_pick_lists(key, part):

    def one_list(list_key):
        key_full, key_order, key_rows, key_shuffle = jax.random.split(list_key, 4)
        full_block = jax.random.randint(key_full, (), 0, N_EXPERT)
        order_ids = jax.random.permutation(key_order, N_EXPERT * SLOT).astype(jnp.int32)
        position = jnp.arange(N_EXPERT * SLOT, dtype=jnp.int32)
        score = jnp.where(position // SLOT == full_block, position - N_EXPERT * SLOT, order_ids)
        taken = jnp.argsort(score, stable=True)[:CAP].astype(jnp.int32)
        block_ids = taken // SLOT
        slot_ids = taken - block_ids * SLOT
        row_tables = jax.vmap(lambda row_key: jax.random.permutation(row_key, TOK_DEV).astype(jnp.int32))(jax.random.split(key_rows, N_EXPERT))
        chosen_rows = row_tables[block_ids, slot_ids]
        chosen = block_ids * TOK_DEV + chosen_rows
        shuffle = jax.random.permutation(key_shuffle, CAP)
        return chosen[shuffle].astype(jnp.int32)
    list_keys = jax.random.split(jax.random.fold_in(key, 17), N_DP * EXPERTS)
    return jax.vmap(one_list)(list_keys).reshape(N_DP, EXPERTS, CAP)


def block_levels(own_key, dims, shards, low, top_value):
    def one(dim, shards_of):
        heights = jax.random.uniform(jax.random.fold_in(jax.random.fold_in(own_key, 6), dim), (shards_of,), jnp.float32, low / len(shards), top_value / len(shards))
        return jnp.repeat(jnp.exp(heights), dims[dim] // shards_of).reshape((-1,) + (1,) * (len(dims) - dim - 1))

    factor_of = one(*shards[0])
    for cut in shards[1:]:
        factor_of = factor_of * one(*cut)
    return factor_of


def noise(stream_key, extent, width, reach, cuts=(), held_as=jnp.bfloat16):
    values = width * jax.random.normal(stream_key, extent, jnp.float32)
    if cuts:
        values = values * block_levels(stream_key, extent, cuts, -0.22, 0.18)
    return jnp.clip(values, -reach, reach).astype(held_as)


def setup_inputs(seed: int = 0) -> dict:
    key_list = jax.random.split(jax.random.key(seed), 8)
    return {
        "tokens": noise(key_list[0], (TOKENS, D), 1.0, 6.0, ((0, 32),)),
        "cotangent": noise(key_list[1], (TOKENS, D), 1.0, 6.0, ((0, 32),)),
        "pick_lists": draw_pick_lists(jax.random.fold_in(key_list[7], 71), 0),
        "combine": jnp.clip(0.1 + 0.9 * jax.random.uniform(key_list[3], (N_DP, EXPERTS, CAP), jnp.float32) ** block_levels(key_list[3], (N_DP, EXPERTS, CAP), ((0, 2),), -0.2, 0.2), 0.1, 1.0),
        "w_gate": noise(key_list[4], (EXPERTS, FF, D), D ** -0.5, 0.1875, ((0, 16), (1, 2))),
        "w_up": noise(key_list[5], (EXPERTS, FF, D), D ** -0.5, 0.1875, ((0, 16), (1, 2))),
        "w_down": noise(key_list[6], (EXPERTS, FF, D), FF ** -0.5, 0.1875, ((0, 16), (1, 2))),
    }


def silu_parts(gate_pre):
    sigma_gate = jax.nn.sigmoid(gate_pre)
    return gate_pre * sigma_gate, sigma_gate


def blocked_sum(left_parts, right_parts):
    parts = jnp.einsum("rbf,bfd->brd", left_parts.astype(jnp.float32), right_parts.astype(jnp.float32))
    parts = parts.astype(jnp.bfloat16)
    parts = lax.optimization_barrier(parts)
    return jnp.sum(parts.astype(jnp.float32), axis=0).astype(jnp.bfloat16)


def reference(tokens, cotangent, pick_lists, combine, w_gate, w_up, w_down):
    tok_rep = tokens.reshape(N_DP, TOKENS_REP, D)
    cot_rep = cotangent.reshape(N_DP, TOKENS_REP, D)
    replica = jnp.arange(N_DP, dtype=jnp.int32)[:, None]
    block_width = FF // N_DP
    rows_all = N_DP * CAP

    def one_expert(inputs):
        chosen_ids, weights, gate_w, up_w, down_w = inputs
        chosen = tok_rep[replica, chosen_ids].reshape(rows_all, D)
        weighted = (weights[:, :, None] * cot_rep[replica, chosen_ids].astype(jnp.float32)).astype(jnp.bfloat16).reshape(rows_all, D)
        gate_pre = jnp.dot(chosen, gate_w.T, preferred_element_type=jnp.float32)
        up_pre = jnp.dot(chosen, up_w.T, preferred_element_type=jnp.float32)
        silu_gate, sigma_gate = silu_parts(gate_pre)
        hidden = (silu_gate * up_pre).astype(jnp.bfloat16)
        expert_out = blocked_sum(hidden.reshape(rows_all, N_DP, block_width), down_w.reshape(N_DP, block_width, D))
        d_hidden = jnp.dot(weighted, down_w.T, preferred_element_type=jnp.float32)
        d_gate = (d_hidden * up_pre * sigma_gate * (1.0 + gate_pre * (1.0 - sigma_gate))).astype(jnp.bfloat16)
        d_up = (d_hidden * silu_gate).astype(jnp.bfloat16)
        gate_parts = jnp.einsum("rbf,bfd->brd", d_gate.reshape(rows_all, N_DP, block_width).astype(jnp.float32), gate_w.reshape(N_DP, block_width, D).astype(jnp.float32))
        up_parts = jnp.einsum("rbf,bfd->brd", d_up.reshape(rows_all, N_DP, block_width).astype(jnp.float32), up_w.reshape(N_DP, block_width, D).astype(jnp.float32))
        back_parts = lax.optimization_barrier((gate_parts + up_parts).astype(jnp.bfloat16))
        d_chosen = jnp.sum(back_parts.astype(jnp.float32), axis=0).astype(jnp.bfloat16)
        grad_gate = jnp.dot(d_gate.T, chosen, preferred_element_type=jnp.float32).astype(jnp.bfloat16)
        grad_up = jnp.dot(d_up.T, chosen, preferred_element_type=jnp.float32).astype(jnp.bfloat16)
        grad_down = jnp.dot(hidden.T, weighted, preferred_element_type=jnp.float32).astype(jnp.bfloat16)
        return expert_out.reshape(N_DP, CAP, D), d_chosen.reshape(N_DP, CAP, D), grad_gate, grad_up, grad_down

    outputs = lax.map(one_expert, (jnp.swapaxes(pick_lists, 0, 1), jnp.swapaxes(combine, 0, 1), w_gate, w_up, w_down))
    expert_out, d_chosen, grad_gate, grad_up, grad_down = outputs
    replica_three = jnp.arange(N_DP, dtype=jnp.int32)[:, None, None]
    out_terms = combine[:, :, :, None] * jnp.swapaxes(expert_out, 0, 1).astype(jnp.float32)
    layer_out = jnp.zeros((N_DP, TOKENS_REP, D), jnp.float32).at[replica_three, pick_lists].add(out_terms)
    back_terms = jnp.swapaxes(d_chosen, 0, 1).astype(jnp.float32)
    tokens_grad = jnp.zeros((N_DP, TOKENS_REP, D), jnp.float32).at[replica_three, pick_lists].add(back_terms)
    layer_out = layer_out.reshape(TOKENS, D).astype(jnp.bfloat16)
    tokens_grad = tokens_grad.reshape(TOKENS, D).astype(jnp.bfloat16)
    return (layer_out, tokens_grad, grad_gate, grad_up, grad_down)
```

```python
import functools

import jax
import jax.numpy as jnp
from jax import lax
from jax.experimental import pallas as pl
from jax.experimental.pallas import tpu as pltpu
from jax.sharding import PartitionSpec as P

MESH = pl.DeviceIdType.MESH
BF16 = jnp.bfloat16
F32 = jnp.float32
NN = (((1,), (0,)), ((), ()))
NT = (((1,), (1,)), ((), ()))
TN = (((0,), (0,)), ((), ()))


def dot(a, b, dims=NN):
    return lax.dot_general(a, b, dims, preferred_element_type=F32)


def layer_kernel(
    n_dp, n_e, n_c, slot_rows,
    tok_ref, cot_ref, list_ref, comb_ref, wg_hbm, wu_hbm, wd_hbm,
    out_ref, back_ref, gg_hbm, gu_hbm, gd_hbm,
    list_two, comb_two, wg, wu, wd, gg, gu, gd,
    send, recv, rows, part_send, part_own, part_recv, ret_send, ret_recv,
    gate_acc, up_acc, hid, dgate, dup,
    w_sem, g_sem, a2a_ss, a2a_rs, x_ss, x_rs, red_ss, red_rs, ret_ss, ret_rs,
):
    my_dp = lax.axis_index("dp")
    me = lax.axis_index("expert")
    tok_rows, feat = tok_ref.shape
    capacity = list_ref.shape[1]
    ff = wg.shape[0]
    width = feat // n_c
    peers = n_e - 1
    others = n_dp - 1
    padded = n_e * slot_rows
    sent = peers * slot_rows

    barrier = pltpu.get_barrier_semaphore()

    def greet_expert(k, carry):
        pl.semaphore_signal(
            barrier, inc=1, device_id=(my_dp, lax.rem(me + 1 + k, n_e)), device_id_type=MESH
        )
        return carry

    lax.fori_loop(0, peers, greet_expert, 0)
    for q in range(others):
        pl.semaphore_signal(
            barrier, inc=1, device_id=(lax.rem(my_dp + 1 + q, n_dp), me), device_id_type=MESH
        )

    loads = [
        pltpu.make_async_copy(hbm, vmem, w_sem.at[i])
        for i, (hbm, vmem) in enumerate(((wg_hbm, wg), (wu_hbm, wu), (wd_hbm, wd)))
    ]
    for load in loads:
        load.start()

    list_two[0:n_e, :] = list_ref[...]
    list_two[n_e : 2 * n_e, :] = list_ref[...]
    comb_two[0:n_e, :] = comb_ref[...]
    comb_two[n_e : 2 * n_e, :] = comb_ref[...]
    copies = max(1, 128 // n_e)
    list_rel = list_two[pl.ds(me + 1, n_e), :].astype(F32)
    comb_rel = comb_two[pl.ds(me + 1, n_e), :]
    list_t = jnp.concatenate([list_rel] * copies, axis=0).T
    comb_t = jnp.concatenate([comb_rel] * copies, axis=0).T
    base = (me * tok_rows).astype(F32)
    token_id = lax.broadcasted_iota(jnp.int32, (1, tok_rows), 1).astype(F32) + base
    member_rows, weight_rows = [], []
    for k in range(n_e):
        same = list_t[:, k : k + 1] == token_id
        member_rows.append(jnp.sum(jnp.where(same, 1.0, 0.0), axis=0, keepdims=True))
        weight_rows.append(
            jnp.sum(jnp.where(same, comb_t[:, k : k + 1], 0.0), axis=0, keepdims=True)
        )
    member = jnp.concatenate(member_rows, axis=0)
    t_from = lax.broadcasted_iota(jnp.int32, (tok_rows, tok_rows), 0)
    t_to = lax.broadcasted_iota(jnp.int32, (tok_rows, tok_rows), 1)
    before = jnp.where(t_from < t_to, 1.0, 0.0).astype(BF16)
    rank = dot(member.astype(BF16), before)
    rank = jnp.where(member > 0.0, rank, -1.0)
    slot_id = lax.broadcasted_iota(jnp.int32, (slot_rows, tok_rows), 0).astype(F32)
    hits = [slot_id == rank[k : k + 1, :] for k in range(n_e)]
    pick = jnp.concatenate([jnp.where(h, 1.0, 0.0) for h in hits], axis=0)
    pick_w = jnp.concatenate(
        [jnp.where(h, weight_rows[k], 0.0) for k, h in enumerate(hits)], axis=0
    )
    pick_b = pick.astype(BF16)
    row_weight = jnp.sum(pick_w, axis=1, keepdims=True)

    def to_experts(a, c):
        def step(k, carry):
            span = pl.ds(pl.multiple_of(k * slot_rows, 16), slot_rows)
            pltpu.make_async_remote_copy(
                src_ref=send.at[a, c, span],
                dst_ref=recv.at[a, c, span],
                send_sem=a2a_ss.at[a, c],
                recv_sem=a2a_rs.at[a, c],
                device_id=(my_dp, lax.rem(me + 1 + k, n_e)),
                device_id_type=MESH,
            ).start()
            return carry

        lax.fori_loop(0, peers, step, 0)

    def to_sources(a, c):
        def step(k, carry):
            span = pl.ds(pl.multiple_of(k * slot_rows, 16), slot_rows)
            pltpu.make_async_remote_copy(
                src_ref=ret_send.at[a, c, span],
                dst_ref=ret_recv.at[a, c, span],
                send_sem=ret_ss.at[a, c],
                recv_sem=ret_rs.at[a, c],
                device_id=(my_dp, lax.rem(me + (n_e - 1) - k, n_e)),
                device_id_type=MESH,
            ).start()
            return carry

        lax.fori_loop(0, peers, step, 0)

    def whole(src, dst, ss, rs, a, c, count):
        return pltpu.make_async_remote_copy(
            src_ref=src.at[a, c, 0:count],
            dst_ref=dst.at[a, c, 0:count],
            send_sem=ss.at[a, c],
            recv_sem=rs.at[a, c],
            device_id=(my_dp, lax.rem(me + 1, n_e)),
            device_id_type=MESH,
        )

    def a2a_all(a, c):
        return whole(send, recv, a2a_ss, a2a_rs, a, c, sent)

    def ret_all(a, c):
        return whole(ret_send, ret_recv, ret_ss, ret_rs, a, c, sent)

    def x_all(a, c):
        return whole(rows, rows, x_ss, x_rs, a, c, others * capacity)

    def red_all(a, c):
        return whole(part_send, part_recv, red_ss, red_rs, a, c, others * capacity)

    for a in range(2):
        for c in range(n_c):
            cols = slice(c * width, (c + 1) * width)
            if a == 0:
                block = dot(pick_b, tok_ref[:, cols]).astype(BF16)
            else:
                block = (row_weight * dot(pick_b, cot_ref[:, cols])).astype(BF16)
            send[a, c] = block[0:sent]
            recv[a, c, sent:padded] = block[sent:padded]
            if a == 0 and c == 0:
                pl.semaphore_wait(barrier, peers + others)
            to_experts(a, c)

    lane = lax.broadcasted_iota(jnp.int32, (1, padded), 1).astype(F32)
    lane_k = jnp.floor((lane + 0.5) * (1.0 / slot_rows))
    lane_s = lane - lane_k * slot_rows
    source = me.astype(F32) - 1.0 - lane_k
    source = jnp.where(source < 0.0, source + n_e, source)
    own_list = list_t[:, n_e - 1 : n_e]
    low = source * tok_rows
    first = jnp.sum(jnp.where(own_list < low, 1.0, 0.0), axis=0, keepdims=True)
    last = jnp.sum(jnp.where(own_list < low + tok_rows, 1.0, 0.0), axis=0, keepdims=True)
    place = jnp.where(lane_s < last - first, first + lane_s, -1.0)
    row_id = lax.broadcasted_iota(jnp.int32, (capacity, padded), 0).astype(F32)
    pack = jnp.where(row_id == place, 1.0, 0.0)
    pack_b = pack.astype(BF16)
    unpack_b = pack.T.astype(BF16)
    pick_t = pick.T.astype(BF16)
    pick_wt = pick_w.T
    wt_high = pick_wt.astype(BF16)
    wt_low = (pick_wt - wt_high.astype(F32)).astype(BF16)

    def share(a, c):
        a2a_all(a, c).wait_recv()
        rows[a, c, others * capacity :] = dot(pack_b, recv[a, c]).astype(BF16)
        for q in range(others):
            pltpu.make_async_remote_copy(
                src_ref=rows.at[a, c, pl.ds(others * capacity, capacity)],
                dst_ref=rows.at[a, c, pl.ds(q * capacity, capacity)],
                send_sem=x_ss.at[a, c],
                recv_sem=x_rs.at[a, c],
                device_id=(lax.rem(my_dp + 1 + q, n_dp), me),
                device_id_type=MESH,
            ).start()

    def reduce_start(a, c, part):
        part = part.astype(BF16)
        part_send[a, c] = part[0 : others * capacity]
        part_own[a, c] = part[others * capacity :]
        for q in range(others):
            pltpu.make_async_remote_copy(
                src_ref=part_send.at[a, c, pl.ds(q * capacity, capacity)],
                dst_ref=part_recv.at[a, c, pl.ds(q * capacity, capacity)],
                send_sem=red_ss.at[a, c],
                recv_sem=red_rs.at[a, c],
                device_id=(lax.rem(my_dp + (n_dp - 1) - q, n_dp), me),
                device_id_type=MESH,
            ).start()

    def give_back(a, c):
        red_all(a, c).wait_recv()
        total = part_own[a, c].astype(F32)
        for q in range(others):
            total = total + part_recv[a, c, q * capacity : (q + 1) * capacity].astype(F32)
        slots = dot(unpack_b, total.astype(BF16)).astype(BF16)
        ret_send[a, c] = slots[0:sent]
        ret_recv[a, c, sent:padded] = slots[sent:padded]
        to_sources(a, c)

    h_step = min(256, ff)
    h_cuts = [slice(h, h + h_step) for h in range(0, ff, h_step)]

    for c in range(n_c):
        share(0, c)
    for load in loads:
        load.wait()
    for c in range(n_c):
        x_all(0, c).wait_recv()
        cols = slice(c * width, (c + 1) * width)
        for h in h_cuts:
            gate = dot(rows[0, c], wg[h, cols], NT)
            up = dot(rows[0, c], wu[h, cols], NT)
            if c > 0:
                gate = gate + gate_acc[:, h]
                up = up + up_acc[:, h]
            if c < n_c - 1:
                gate_acc[:, h] = gate
                up_acc[:, h] = up
            else:
                sigma = jax.nn.sigmoid(gate)
                silu = gate * sigma
                hid[:, h] = (silu * up).astype(BF16)
                gate_acc[:, h] = up * sigma * (1.0 + gate * (1.0 - sigma))
                up_acc[:, h] = silu
    for c in range(n_c):
        reduce_start(0, c, dot(hid[...], wd[:, c * width : (c + 1) * width]))
    share(1, 0)
    give_back(0, 0)
    for c in range(1, n_c):
        share(1, c)
        give_back(0, c)

    for h in h_cuts:
        d_hidden = None
        for c in range(n_c):
            if h.start == 0:
                x_all(1, c).wait_recv()
            term = dot(rows[1, c], wd[h, c * width : (c + 1) * width], NT)
            d_hidden = term if d_hidden is None else d_hidden + term
        dgate[:, h] = (d_hidden * gate_acc[:, h]).astype(BF16)
        dup[:, h] = (d_hidden * up_acc[:, h]).astype(BF16)
    for c in range(n_c):
        cols = slice(c * width, (c + 1) * width)
        reduce_start(1, c, dot(dgate[...], wg[:, cols]) + dot(dup[...], wu[:, cols]))

    def weight_grad(c, left, a, grad):
        cols = slice(c * width, (c + 1) * width)
        for h in h_cuts:
            grad[h, cols] = dot(left[:, h], rows[a, c], TN).astype(BF16)

    stores = [
        pltpu.make_async_copy(vmem, hbm, g_sem.at[i])
        for i, (vmem, hbm) in enumerate(((gg, gg_hbm), (gu, gu_hbm), (gd, gd_hbm)))
    ]
    for c in range(n_c):
        weight_grad(c, hid, 1, gd)
    stores[2].start()
    for c in range(n_c):
        give_back(1, c)
    for c in range(n_c):
        weight_grad(c, dgate, 0, gg)
    stores[0].start()
    for c in range(n_c):
        weight_grad(c, dup, 0, gu)
    stores[1].start()

    for c in range(n_c):
        cols = slice(c * width, (c + 1) * width)
        ret_all(0, c).wait_recv()
        got = ret_recv[0, c]
        out_ref[:, cols] = (dot(wt_high, got) + dot(wt_low, got)).astype(BF16)
    for c in range(n_c):
        cols = slice(c * width, (c + 1) * width)
        ret_all(1, c).wait_recv()
        back_ref[:, cols] = dot(pick_t, ret_recv[1, c]).astype(BF16)
    for store in stores:
        store.wait()
    for a in range(2):
        for c in range(n_c):
            a2a_all(a, c).wait_send()
            x_all(a, c).wait_send()
            red_all(a, c).wait_send()
            ret_all(a, c).wait_send()


def per_device(n_dp, n_e, tokens, cotangent, pick_lists, combine, w_gate, w_up, w_down):
    tok_rows, feat = tokens.shape
    capacity = pick_lists.shape[2]
    ff = w_gate.shape[1]
    slot_count = max(2, (2 * capacity + n_e - 1) // n_e)
    slot_rows = (slot_count + 15) // 16 * 16
    n_c = 2
    width = feat // n_c
    padded = n_e * slot_rows
    sent = padded - slot_rows
    total_rows = n_dp * capacity
    other_rows = total_rows - capacity
    vmem = pl.BlockSpec(memory_space=pltpu.VMEM)
    hbm = pl.BlockSpec(memory_space=pl.ANY)
    grad = jax.ShapeDtypeStruct((ff, feat), BF16)
    sems = pltpu.SemaphoreType.DMA((2, n_c))
    outs = pl.pallas_call(
        functools.partial(layer_kernel, n_dp, n_e, n_c, slot_rows),
        out_shape=(
            jax.ShapeDtypeStruct((tok_rows, feat), BF16),
            jax.ShapeDtypeStruct((tok_rows, feat), BF16),
            grad,
            grad,
            grad,
        ),
        in_specs=[vmem] * 4 + [hbm] * 3,
        out_specs=(vmem, vmem, hbm, hbm, hbm),
        scratch_shapes=[
            pltpu.VMEM((2 * n_e, capacity), jnp.int32),
            pltpu.VMEM((2 * n_e, capacity), F32),
        ]
        + [pltpu.VMEM((ff, feat), BF16)] * 6
        + [
            pltpu.VMEM((2, n_c, sent, width), BF16),
            pltpu.VMEM((2, n_c, padded, width), BF16),
            pltpu.VMEM((2, n_c, total_rows, width), BF16),
            pltpu.VMEM((2, n_c, other_rows, width), BF16),
            pltpu.VMEM((2, n_c, capacity, width), BF16),
            pltpu.VMEM((2, n_c, other_rows, width), BF16),
            pltpu.VMEM((2, n_c, sent, width), BF16),
            pltpu.VMEM((2, n_c, padded, width), BF16),
            pltpu.VMEM((total_rows, ff), F32),
            pltpu.VMEM((total_rows, ff), F32),
        ]
        + [pltpu.VMEM((total_rows, ff), BF16)] * 3
        + [pltpu.SemaphoreType.DMA((3,))] * 2
        + [sems] * 8,
        compiler_params=pltpu.CompilerParams(
            collective_id=0, has_side_effects=True, vmem_limit_bytes=56 * 2**20
        ),
        cost_estimate=pl.CostEstimate(
            flops=18 * total_rows * ff * feat,
            bytes_accessed=12 * ff * feat + 8 * tok_rows * feat,
            transcendentals=total_rows * ff,
        ),
        name="expert_layer",
    )(tokens, cotangent, pick_lists[0], combine[0], w_gate[0], w_up[0], w_down[0])
    layer_out, tokens_grad, grad_gate, grad_up, grad_down = outs
    return (layer_out, tokens_grad, grad_gate[None], grad_up[None], grad_down[None])


def solution(mesh):
    placed = (
        P(("dp", "expert"), None),
        P(("dp", "expert"), None),
        P("dp", None, None),
        P("dp", None, None),
        P("expert", "dp", None),
        P("expert", "dp", None),
        P("expert", "dp", None),
    )
    return jax.shard_map(
        functools.partial(per_device, mesh.shape["dp"], mesh.shape["expert"]),
        mesh=mesh,
        in_specs=placed,
        out_specs=(
            P(("dp", "expert"), None),
            P(("dp", "expert"), None),
            P("expert", "dp", None),
            P("expert", "dp", None),
            P("expert", "dp", None),
        ),
        check_vma=False,
    )
```

```python
import functools

import jax
import jax.numpy as jnp
from jax import lax
from jax.experimental import pallas as pl
from jax.experimental.pallas import tpu as pltpu
from jax.sharding import PartitionSpec as P

MESH = pl.DeviceIdType.MESH
BF16 = jnp.bfloat16
F32 = jnp.float32
NN = (((1,), (0,)), ((), ()))
NT = (((1,), (1,)), ((), ()))
TN = (((0,), (0,)), ((), ()))


def dot(a, b, dims=NN):
    return lax.dot_general(a, b, dims, preferred_element_type=F32)


def layer_kernel(
    n_dp, n_e, n_c, slot_rows,
    tok_hbm, cot_hbm, list_hbm, comb_hbm, wg_hbm, wu_hbm, wd_hbm,
    out_ref, back_ref, gg, gu, gd,
    list_two, comb_two, tok_ref, cot_ref, wg, wu, wd,
    send, recv, rows, part_send, part_own, part_recv, ret_send, ret_recv,
    gate_acc, up_acc, hid, dgate, dup,
    w_sem, a2a_ss, a2a_rs, x_ss, x_rs, red_ss, red_rs, ret_ss, ret_rs,
):
    my_dp = lax.axis_index("dp")
    me = lax.axis_index("expert")
    tok_rows, feat = tok_ref.shape
    capacity = list_two.shape[1]
    ff = wg.shape[0]
    width = feat // n_c
    peers = n_e - 1
    others = n_dp - 1
    padded = n_e * slot_rows
    sent = peers * slot_rows

    barrier = pltpu.get_barrier_semaphore()

    def greet_expert(k, carry):
        pl.semaphore_signal(
            barrier, inc=1, device_id=(my_dp, lax.rem(me + 1 + k, n_e)), device_id_type=MESH
        )
        return carry

    lax.fori_loop(0, peers, greet_expert, 0)
    for q in range(others):
        pl.semaphore_signal(
            barrier, inc=1, device_id=(lax.rem(my_dp + 1 + q, n_dp), me), device_id_type=MESH
        )

    early = [
        pltpu.make_async_copy(hbm, vmem, w_sem.at[i])
        for i, (hbm, vmem) in enumerate(
            (
                (list_hbm, list_two.at[pl.ds(0, n_e)]),
                (list_hbm, list_two.at[pl.ds(n_e, n_e)]),
                (comb_hbm, comb_two.at[pl.ds(0, n_e)]),
                (comb_hbm, comb_two.at[pl.ds(n_e, n_e)]),
                (tok_hbm, tok_ref),
                (cot_hbm, cot_ref),
            )
        )
    ]
    loads = [
        pltpu.make_async_copy(hbm, vmem, w_sem.at[6 + i])
        for i, (hbm, vmem) in enumerate(((wg_hbm, wg), (wu_hbm, wu), (wd_hbm, wd)))
    ]
    for load in early + loads:
        load.start()
    for load in early[:4]:
        load.wait()

    copies = max(1, 128 // n_e)
    list_rel = list_two[pl.ds(me + 1, n_e), :].astype(F32)
    comb_rel = comb_two[pl.ds(me + 1, n_e), :]
    list_t = jnp.concatenate([list_rel] * copies, axis=0).T
    comb_t = jnp.concatenate([comb_rel] * copies, axis=0).T
    base = (me * tok_rows).astype(F32)
    token_id = lax.broadcasted_iota(jnp.int32, (1, tok_rows), 1).astype(F32) + base
    member_rows, weight_rows = [], []
    for k in range(n_e):
        same = list_t[:, k : k + 1] == token_id
        member_rows.append(jnp.sum(jnp.where(same, 1.0, 0.0), axis=0, keepdims=True))
        weight_rows.append(
            jnp.sum(jnp.where(same, comb_t[:, k : k + 1], 0.0), axis=0, keepdims=True)
        )
    member = jnp.concatenate(member_rows, axis=0)
    t_from = lax.broadcasted_iota(jnp.int32, (tok_rows, tok_rows), 0)
    t_to = lax.broadcasted_iota(jnp.int32, (tok_rows, tok_rows), 1)
    before = jnp.where(t_from < t_to, 1.0, 0.0).astype(BF16)
    rank = dot(member.astype(BF16), before)
    rank = jnp.where(member > 0.0, rank, -1.0)
    slot_id = lax.broadcasted_iota(jnp.int32, (slot_rows, tok_rows), 0).astype(F32)
    hits = [slot_id == rank[k : k + 1, :] for k in range(n_e)]
    pick = jnp.concatenate([jnp.where(h, 1.0, 0.0) for h in hits], axis=0)
    pick_w = jnp.concatenate(
        [jnp.where(h, weight_rows[k], 0.0) for k, h in enumerate(hits)], axis=0
    )
    pick_b = pick.astype(BF16)
    row_weight = jnp.sum(pick_w, axis=1, keepdims=True)

    def to_experts(a, c):
        def step(i, carry):
            k = lax.rem(i * (peers // 2), peers)
            span = pl.ds(pl.multiple_of(k * slot_rows, 16), slot_rows)
            pltpu.make_async_remote_copy(
                src_ref=send.at[a, c, span],
                dst_ref=recv.at[a, c, span],
                send_sem=a2a_ss.at[a, c],
                recv_sem=a2a_rs.at[a, c],
                device_id=(my_dp, lax.rem(me + 1 + k, n_e)),
                device_id_type=MESH,
            ).start()
            return carry

        lax.fori_loop(0, peers, step, 0)

    def to_sources(a, c):
        def step(i, carry):
            k = lax.rem(i * (peers // 2), peers)
            span = pl.ds(pl.multiple_of(k * slot_rows, 16), slot_rows)
            pltpu.make_async_remote_copy(
                src_ref=ret_send.at[a, c, span],
                dst_ref=ret_recv.at[a, c, span],
                send_sem=ret_ss.at[a, c],
                recv_sem=ret_rs.at[a, c],
                device_id=(my_dp, lax.rem(me + (n_e - 1) - k, n_e)),
                device_id_type=MESH,
            ).start()
            return carry

        lax.fori_loop(0, peers, step, 0)

    def whole(src, dst, ss, rs, a, c, count):
        return pltpu.make_async_remote_copy(
            src_ref=src.at[a, c, 0:count],
            dst_ref=dst.at[a, c, 0:count],
            send_sem=ss.at[a, c],
            recv_sem=rs.at[a, c],
            device_id=(my_dp, lax.rem(me + 1, n_e)),
            device_id_type=MESH,
        )

    def a2a_all(a, c):
        return whole(send, recv, a2a_ss, a2a_rs, a, c, sent)

    def ret_all(a, c):
        return whole(ret_send, ret_recv, ret_ss, ret_rs, a, c, sent)

    def x_all(a, c):
        return whole(rows, rows, x_ss, x_rs, a, c, others * capacity)

    def red_all(a, c):
        return whole(part_send, part_recv, red_ss, red_rs, a, c, others * capacity)

    def dispatch(a, c):
        cols = slice(c * width, (c + 1) * width)
        if a == 0:
            block = dot(pick_b, tok_ref[:, cols]).astype(BF16)
        else:
            block = (row_weight * dot(pick_b, cot_ref[:, cols])).astype(BF16)
        send[a, c] = block[0:sent]
        recv[a, c, sent:padded] = block[sent:padded]
        if a == 0 and c == 0:
            pl.semaphore_wait(barrier, peers + others)
        to_experts(a, c)

    early[4].wait()
    for c in range(n_c):
        dispatch(0, c)
    early[5].wait()
    for c in range(2):
        dispatch(1, c)

    lane = lax.broadcasted_iota(jnp.int32, (1, padded), 1).astype(F32)
    lane_k = jnp.floor((lane + 0.5) * (1.0 / slot_rows))
    lane_s = lane - lane_k * slot_rows
    source = me.astype(F32) - 1.0 - lane_k
    source = jnp.where(source < 0.0, source + n_e, source)
    own_list = list_t[:, n_e - 1 : n_e]
    low = source * tok_rows
    first = jnp.sum(jnp.where(own_list < low, 1.0, 0.0), axis=0, keepdims=True)
    last = jnp.sum(jnp.where(own_list < low + tok_rows, 1.0, 0.0), axis=0, keepdims=True)
    place = jnp.where(lane_s < last - first, first + lane_s, -1.0)
    row_id = lax.broadcasted_iota(jnp.int32, (capacity, padded), 0).astype(F32)
    pack = jnp.where(row_id == place, 1.0, 0.0)
    pack_b = pack.astype(BF16)
    unpack_b = pack.T.astype(BF16)
    pick_t = pick.T.astype(BF16)
    pick_wt = pick_w.T
    wt_high = pick_wt.astype(BF16)
    wt_low = (pick_wt - wt_high.astype(F32)).astype(BF16)

    def share(a, c):
        a2a_all(a, c).wait_recv()
        rows[a, c, others * capacity :] = dot(pack_b, recv[a, c]).astype(BF16)
        for q in range(others):
            pltpu.make_async_remote_copy(
                src_ref=rows.at[a, c, pl.ds(others * capacity, capacity)],
                dst_ref=rows.at[a, c, pl.ds(q * capacity, capacity)],
                send_sem=x_ss.at[a, c],
                recv_sem=x_rs.at[a, c],
                device_id=(lax.rem(my_dp + 1 + q, n_dp), me),
                device_id_type=MESH,
            ).start()

    def reduce_start(a, c, part):
        part = part.astype(BF16)
        part_send[a, c] = part[0 : others * capacity]
        part_own[a, c] = part[others * capacity :]
        for q in range(others):
            pltpu.make_async_remote_copy(
                src_ref=part_send.at[a, c, pl.ds(q * capacity, capacity)],
                dst_ref=part_recv.at[a, c, pl.ds(q * capacity, capacity)],
                send_sem=red_ss.at[a, c],
                recv_sem=red_rs.at[a, c],
                device_id=(lax.rem(my_dp + (n_dp - 1) - q, n_dp), me),
                device_id_type=MESH,
            ).start()

    def give_back(a, c):
        red_all(a, c).wait_recv()
        total = part_own[a, c].astype(F32)
        for q in range(others):
            total = total + part_recv[a, c, q * capacity : (q + 1) * capacity].astype(F32)
        slots = dot(unpack_b, total.astype(BF16)).astype(BF16)
        ret_send[a, c] = slots[0:sent]
        ret_recv[a, c, sent:padded] = slots[sent:padded]
        to_sources(a, c)

    h_step = min(256, ff)
    h_cuts = [slice(h, h + h_step) for h in range(0, ff, h_step)]

    for c in range(n_c):
        share(0, c)
        if c + 2 < n_c:
            dispatch(1, c + 2)
    for load in loads:
        load.wait()
    for c in range(n_c):
        x_all(0, c).wait_recv()
        cols = slice(c * width, (c + 1) * width)
        for h in h_cuts:
            gate = dot(rows[0, c], wg[h, cols], NT)
            up = dot(rows[0, c], wu[h, cols], NT)
            if c > 0:
                gate = gate + gate_acc[:, h]
                up = up + up_acc[:, h]
            if c < n_c - 1:
                gate_acc[:, h] = gate
                up_acc[:, h] = up
            else:
                sigma = jax.nn.sigmoid(gate)
                silu = gate * sigma
                hid[:, h] = (silu * up).astype(BF16)
                gate_acc[:, h] = up * sigma * (1.0 + gate * (1.0 - sigma))
                up_acc[:, h] = silu
    for c in range(n_c):
        reduce_start(0, c, dot(hid[...], wd[:, c * width : (c + 1) * width]))
    share(1, 0)
    give_back(0, 0)
    for c in range(1, n_c):
        share(1, c)
        give_back(0, c)

    for h in h_cuts:
        d_hidden = None
        for c in range(n_c):
            if h.start == 0:
                x_all(1, c).wait_recv()
            term = dot(rows[1, c], wd[h, c * width : (c + 1) * width], NT)
            d_hidden = term if d_hidden is None else d_hidden + term
        dgate[:, h] = (d_hidden * gate_acc[:, h]).astype(BF16)
        dup[:, h] = (d_hidden * up_acc[:, h]).astype(BF16)
    for c in range(n_c):
        cols = slice(c * width, (c + 1) * width)
        reduce_start(1, c, dot(dgate[...], wg[:, cols]) + dot(dup[...], wu[:, cols]))

    def weight_grad(c, left, a, grad):
        cols = slice(c * width, (c + 1) * width)
        for h in h_cuts:
            grad[h, cols] = dot(left[:, h], rows[a, c], TN).astype(BF16)

    for c in range(n_c):
        weight_grad(c, hid, 1, gd)
    for c in range(n_c):
        give_back(1, c)
    for c in range(n_c):
        weight_grad(c, dgate, 0, gg)
    for c in range(n_c):
        weight_grad(c, dup, 0, gu)

    for c in range(n_c):
        cols = slice(c * width, (c + 1) * width)
        ret_all(0, c).wait_recv()
        got = ret_recv[0, c]
        out_ref[:, cols] = (dot(wt_high, got) + dot(wt_low, got)).astype(BF16)
    for c in range(n_c):
        cols = slice(c * width, (c + 1) * width)
        ret_all(1, c).wait_recv()
        back_ref[:, cols] = dot(pick_t, ret_recv[1, c]).astype(BF16)
    for a in range(2):
        for c in range(n_c):
            a2a_all(a, c).wait_send()
            x_all(a, c).wait_send()
            red_all(a, c).wait_send()
            ret_all(a, c).wait_send()


def store_kernel(*refs):
    sem = refs[10]
    copies = [pltpu.make_async_copy(refs[i], refs[5 + i], sem.at[i]) for i in range(5)]
    for copy in copies:
        copy.start()
    for copy in copies:
        copy.wait()


def per_device(n_dp, n_e, tokens, cotangent, pick_lists, combine, w_gate, w_up, w_down):
    tok_rows, feat = tokens.shape
    capacity = pick_lists.shape[2]
    ff = w_gate.shape[1]
    slot_count = max(2, (2 * capacity + n_e - 1) // n_e)
    slot_rows = (slot_count + 15) // 16 * 16
    n_c = 4
    width = feat // n_c
    padded = n_e * slot_rows
    sent = padded - slot_rows
    total_rows = n_dp * capacity
    other_rows = total_rows - capacity
    vmem = pl.BlockSpec(memory_space=pltpu.VMEM)
    hbm = pl.BlockSpec(memory_space=pl.ANY)
    grad = jax.ShapeDtypeStruct((ff, feat), BF16)
    sems = pltpu.SemaphoreType.DMA((2, n_c))
    outs = pl.pallas_call(
        functools.partial(layer_kernel, n_dp, n_e, n_c, slot_rows),
        out_shape=(pltpu.VMEM((tok_rows, feat), BF16),) * 2 + (pltpu.VMEM((ff, feat), BF16),) * 3,
        in_specs=[pl.BlockSpec(memory_space=pltpu.HBM)] * 7,
        out_specs=(vmem,) * 5,
        scratch_shapes=[
            pltpu.VMEM((2 * n_e, capacity), jnp.int32),
            pltpu.VMEM((2 * n_e, capacity), F32),
        ]
        + [pltpu.VMEM((tok_rows, feat), BF16)] * 2
        + [pltpu.VMEM((ff, feat), BF16)] * 3
        + [
            pltpu.VMEM((2, n_c, sent, width), BF16),
            pltpu.VMEM((2, n_c, padded, width), BF16),
            pltpu.VMEM((2, n_c, total_rows, width), BF16),
            pltpu.VMEM((2, n_c, other_rows, width), BF16),
            pltpu.VMEM((2, n_c, capacity, width), BF16),
            pltpu.VMEM((2, n_c, other_rows, width), BF16),
            pltpu.VMEM((2, n_c, sent, width), BF16),
            pltpu.VMEM((2, n_c, padded, width), BF16),
            pltpu.VMEM((total_rows, ff), F32),
            pltpu.VMEM((total_rows, ff), F32),
        ]
        + [pltpu.VMEM((total_rows, ff), BF16)] * 3
        + [pltpu.SemaphoreType.DMA((9,))]
        + [sems] * 8,
        compiler_params=pltpu.CompilerParams(
            collective_id=0, has_side_effects=True, vmem_limit_bytes=59 * 2**20
        ),
        cost_estimate=pl.CostEstimate(
            flops=18 * total_rows * ff * feat,
            bytes_accessed=12 * ff * feat + 8 * tok_rows * feat,
            transcendentals=total_rows * ff,
        ),
        name="expert_layer",
    )(tokens, cotangent, pick_lists[0], combine[0], w_gate[0], w_up[0], w_down[0])
    layer_out, tokens_grad, grad_gate, grad_up, grad_down = pl.pallas_call(
        store_kernel,
        out_shape=[jax.ShapeDtypeStruct(o.shape, o.dtype) for o in outs],
        in_specs=[vmem] * 5,
        out_specs=[hbm] * 5,
        scratch_shapes=[pltpu.SemaphoreType.DMA((5,))],
        compiler_params=pltpu.CompilerParams(vmem_limit_bytes=16 * 2**20),
        name="store_results",
    )(*outs)
    return (layer_out, tokens_grad, grad_gate[None], grad_up[None], grad_down[None])


def solution(mesh):
    placed = (
        P(("dp", "expert"), None),
        P(("dp", "expert"), None),
        P("dp", None, None),
        P("dp", None, None),
        P("expert", "dp", None),
        P("expert", "dp", None),
        P("expert", "dp", None),
    )
    return jax.shard_map(
        functools.partial(per_device, mesh.shape["dp"], mesh.shape["expert"]),
        mesh=mesh,
        in_specs=placed,
        out_specs=(
            P(("dp", "expert"), None),
            P(("dp", "expert"), None),
            P("expert", "dp", None),
            P("expert", "dp", None),
            P("expert", "dp", None),
        ),
        check_vma=False,
    )
```

```python
import functools

import jax
import jax.numpy as jnp
from jax import lax
from jax.experimental import pallas as pl
from jax.experimental.pallas import tpu as pltpu
from jax.sharding import PartitionSpec as P

MESH = pl.DeviceIdType.MESH
BF16 = jnp.bfloat16
F32 = jnp.float32
NN = (((1,), (0,)), ((), ()))
NT = (((1,), (1,)), ((), ()))
TN = (((0,), (0,)), ((), ()))


def dot(a, b, dims=NN):
    return lax.dot_general(a, b, dims, preferred_element_type=F32)


def layer_kernel(
    n_dp, n_e, n_c, slot_rows,
    tok_hbm, cot_hbm, list_hbm, comb_hbm, wg_hbm, wu_hbm, wd_hbm,
    out_ref, back_ref, gg, gu, gd,
    list_two, comb_two, tok_ref, cot_ref, wg, wu, wd,
    send, recv, rows, part_send, part_own, part_recv, ret_send, ret_recv,
    gate_acc, up_acc, hid, dgate, dup,
    w_sem, a2a_ss, a2a_rs, x_ss, x_rs, red_ss, red_rs, ret_ss, ret_rs,
):
    my_dp = lax.axis_index("dp")
    me = lax.axis_index("expert")
    tok_rows, feat = tok_ref.shape
    capacity = list_two.shape[1]
    ff = wg.shape[0]
    width = feat // n_c
    peers = n_e - 1
    others = n_dp - 1
    padded = n_e * slot_rows
    sent = peers * slot_rows

    barrier = pltpu.get_barrier_semaphore()

    def greet_expert(k, carry):
        pl.semaphore_signal(
            barrier, inc=1, device_id=(my_dp, lax.rem(me + 1 + k, n_e)), device_id_type=MESH
        )
        return carry

    lax.fori_loop(0, peers, greet_expert, 0)
    for q in range(others):
        pl.semaphore_signal(
            barrier, inc=1, device_id=(lax.rem(my_dp + 1 + q, n_dp), me), device_id_type=MESH
        )

    early = [
        pltpu.make_async_copy(hbm, vmem, w_sem.at[i])
        for i, (hbm, vmem) in enumerate(
            (
                (list_hbm, list_two.at[pl.ds(0, n_e)]),
                (list_hbm, list_two.at[pl.ds(n_e, n_e)]),
                (comb_hbm, comb_two.at[pl.ds(0, n_e)]),
                (comb_hbm, comb_two.at[pl.ds(n_e, n_e)]),
                (tok_hbm, tok_ref),
                (cot_hbm, cot_ref),
            )
        )
    ]
    loads = [
        pltpu.make_async_copy(hbm, vmem, w_sem.at[6 + i])
        for i, (hbm, vmem) in enumerate(((wg_hbm, wg), (wu_hbm, wu), (wd_hbm, wd)))
    ]
    for load in early + loads:
        load.start()
    for load in early[:4]:
        load.wait()

    copies = max(1, 128 // n_e)
    list_rel = list_two[pl.ds(me + 1, n_e), :].astype(F32)
    comb_rel = comb_two[pl.ds(me + 1, n_e), :]
    list_t = jnp.concatenate([list_rel] * copies, axis=0).T
    comb_t = jnp.concatenate([comb_rel] * copies, axis=0).T
    base = (me * tok_rows).astype(F32)
    token_id = lax.broadcasted_iota(jnp.int32, (1, tok_rows), 1).astype(F32) + base
    member_rows = []
    for k in range(n_e):
        same = list_t[:, k : k + 1] == token_id
        member_rows.append(jnp.sum(jnp.where(same, 1.0, 0.0), axis=0, keepdims=True))
    member = jnp.concatenate(member_rows, axis=0)
    t_from = lax.broadcasted_iota(jnp.int32, (tok_rows, tok_rows), 0)
    t_to = lax.broadcasted_iota(jnp.int32, (tok_rows, tok_rows), 1)
    before = jnp.where(t_from < t_to, 1.0, 0.0).astype(BF16)
    rank = dot(member.astype(BF16), before)
    rank = jnp.where(member > 0.0, rank, -1.0)
    slot_id = lax.broadcasted_iota(jnp.int32, (slot_rows, tok_rows), 0).astype(F32)
    hits = [slot_id == rank[k : k + 1, :] for k in range(n_e)]
    pick = jnp.concatenate([jnp.where(h, 1.0, 0.0) for h in hits], axis=0)
    pick_b = pick.astype(BF16)

    def to_experts(a, c):
        def step(i, carry):
            k = lax.rem(i * (peers // 2), peers)
            span = pl.ds(pl.multiple_of(k * slot_rows, 16), slot_rows)
            pltpu.make_async_remote_copy(
                src_ref=send.at[a, c, span],
                dst_ref=recv.at[a, c, span],
                send_sem=a2a_ss.at[a, c],
                recv_sem=a2a_rs.at[a, c],
                device_id=(my_dp, lax.rem(me + 1 + k, n_e)),
                device_id_type=MESH,
            ).start()
            return carry

        lax.fori_loop(0, peers, step, 0)

    def to_sources(a, c):
        def step(i, carry):
            k = lax.rem(i * (peers // 2), peers)
            span = pl.ds(pl.multiple_of(k * slot_rows, 16), slot_rows)
            pltpu.make_async_remote_copy(
                src_ref=ret_send.at[a, c, span],
                dst_ref=ret_recv.at[a, c, span],
                send_sem=ret_ss.at[a, c],
                recv_sem=ret_rs.at[a, c],
                device_id=(my_dp, lax.rem(me + (n_e - 1) - k, n_e)),
                device_id_type=MESH,
            ).start()
            return carry

        lax.fori_loop(0, peers, step, 0)

    def whole(src, dst, ss, rs, a, c, count):
        return pltpu.make_async_remote_copy(
            src_ref=src.at[a, c, 0:count],
            dst_ref=dst.at[a, c, 0:count],
            send_sem=ss.at[a, c],
            recv_sem=rs.at[a, c],
            device_id=(my_dp, lax.rem(me + 1, n_e)),
            device_id_type=MESH,
        )

    def a2a_all(a, c):
        return whole(send, recv, a2a_ss, a2a_rs, a, c, sent)

    def ret_all(a, c):
        return whole(ret_send, ret_recv, ret_ss, ret_rs, a, c, sent)

    def x_all(a, c):
        return whole(rows, rows, x_ss, x_rs, a, c, others * capacity)

    def red_all(a, c):
        return whole(part_send, part_recv, red_ss, red_rs, a, c, others * capacity)

    def dispatch(a, c):
        cols = slice(c * width, (c + 1) * width)
        if a == 0:
            block = dot(pick_b, tok_ref[:, cols]).astype(BF16)
        else:
            block = (row_weight * dot(pick_b, cot_ref[:, cols])).astype(BF16)
        send[a, c] = block[0:sent]
        recv[a, c, sent:padded] = block[sent:padded]
        if a == 0 and c == 0:
            pl.semaphore_wait(barrier, peers + others)
        to_experts(a, c)

    early[4].wait()
    for c in range(n_c):
        dispatch(0, c)
    weight_rows = []
    for k in range(n_e):
        same = list_t[:, k : k + 1] == token_id
        weight_rows.append(
            jnp.sum(jnp.where(same, comb_t[:, k : k + 1], 0.0), axis=0, keepdims=True)
        )
    pick_w = jnp.concatenate(
        [jnp.where(h, weight_rows[k], 0.0) for k, h in enumerate(hits)], axis=0
    )
    row_weight = jnp.sum(pick_w, axis=1, keepdims=True)
    early[5].wait()
    for c in range(2):
        dispatch(1, c)

    lane = lax.broadcasted_iota(jnp.int32, (1, padded), 1).astype(F32)
    lane_k = jnp.floor((lane + 0.5) * (1.0 / slot_rows))
    lane_s = lane - lane_k * slot_rows
    source = me.astype(F32) - 1.0 - lane_k
    source = jnp.where(source < 0.0, source + n_e, source)
    own_list = list_t[:, n_e - 1 : n_e]
    low = source * tok_rows
    first = jnp.sum(jnp.where(own_list < low, 1.0, 0.0), axis=0, keepdims=True)
    last = jnp.sum(jnp.where(own_list < low + tok_rows, 1.0, 0.0), axis=0, keepdims=True)
    place = jnp.where(lane_s < last - first, first + lane_s, -1.0)
    row_id = lax.broadcasted_iota(jnp.int32, (capacity, padded), 0).astype(F32)
    pack = jnp.where(row_id == place, 1.0, 0.0)
    pack_b = pack.astype(BF16)
    unpack_b = pack.T.astype(BF16)
    pick_t = pick.T.astype(BF16)
    pick_wt = pick_w.T
    wt_high = pick_wt.astype(BF16)
    wt_low = (pick_wt - wt_high.astype(F32)).astype(BF16)

    def share(a, c):
        a2a_all(a, c).wait_recv()
        rows[a, c, others * capacity :] = dot(pack_b, recv[a, c]).astype(BF16)
        for q in range(others):
            pltpu.make_async_remote_copy(
                src_ref=rows.at[a, c, pl.ds(others * capacity, capacity)],
                dst_ref=rows.at[a, c, pl.ds(q * capacity, capacity)],
                send_sem=x_ss.at[a, c],
                recv_sem=x_rs.at[a, c],
                device_id=(lax.rem(my_dp + 1 + q, n_dp), me),
                device_id_type=MESH,
            ).start()

    def reduce_start(a, c, part):
        part = part.astype(BF16)
        part_send[a, c] = part[0 : others * capacity]
        part_own[a, c] = part[others * capacity :]
        for q in range(others):
            pltpu.make_async_remote_copy(
                src_ref=part_send.at[a, c, pl.ds(q * capacity, capacity)],
                dst_ref=part_recv.at[a, c, pl.ds(q * capacity, capacity)],
                send_sem=red_ss.at[a, c],
                recv_sem=red_rs.at[a, c],
                device_id=(lax.rem(my_dp + (n_dp - 1) - q, n_dp), me),
                device_id_type=MESH,
            ).start()

    def give_back(a, c):
        red_all(a, c).wait_recv()
        total = part_own[a, c].astype(F32)
        for q in range(others):
            total = total + part_recv[a, c, q * capacity : (q + 1) * capacity].astype(F32)
        slots = dot(unpack_b, total.astype(BF16)).astype(BF16)
        ret_send[a, c] = slots[0:sent]
        ret_recv[a, c, sent:padded] = slots[sent:padded]
        to_sources(a, c)

    h_step = min(256, ff)
    h_cuts = [slice(h, h + h_step) for h in range(0, ff, h_step)]

    for c in range(n_c):
        share(0, c)
        if c + 2 < n_c:
            dispatch(1, c + 2)
    for load in loads:
        load.wait()
    for c in range(n_c):
        x_all(0, c).wait_recv()
        cols = slice(c * width, (c + 1) * width)
        for h in h_cuts:
            gate = dot(rows[0, c], wg[h, cols], NT)
            up = dot(rows[0, c], wu[h, cols], NT)
            if c > 0:
                gate = gate + gate_acc[:, h]
                up = up + up_acc[:, h]
            if c < n_c - 1:
                gate_acc[:, h] = gate
                up_acc[:, h] = up
            else:
                sigma = jax.nn.sigmoid(gate)
                silu = gate * sigma
                hid[:, h] = (silu * up).astype(BF16)
                gate_acc[:, h] = up * sigma * (1.0 + gate * (1.0 - sigma))
                up_acc[:, h] = silu
    for c in range(n_c):
        reduce_start(0, c, dot(hid[...], wd[:, c * width : (c + 1) * width]))
    share(1, 0)
    give_back(0, 0)
    for c in range(1, n_c):
        share(1, c)
        give_back(0, c)

    for h in h_cuts:
        d_hidden = None
        for c in range(n_c):
            if h.start == 0:
                x_all(1, c).wait_recv()
            term = dot(rows[1, c], wd[h, c * width : (c + 1) * width], NT)
            d_hidden = term if d_hidden is None else d_hidden + term
        dgate[:, h] = (d_hidden * gate_acc[:, h]).astype(BF16)
        dup[:, h] = (d_hidden * up_acc[:, h]).astype(BF16)
    for c in range(n_c):
        cols = slice(c * width, (c + 1) * width)
        reduce_start(1, c, dot(dgate[...], wg[:, cols]) + dot(dup[...], wu[:, cols]))

    def weight_grad(c, left, a, grad):
        cols = slice(c * width, (c + 1) * width)
        for h in h_cuts:
            grad[h, cols] = dot(left[:, h], rows[a, c], TN).astype(BF16)

    for c in range(n_c):
        weight_grad(c, hid, 1, gd)
    for c in range(n_c):
        give_back(1, c)
    for c in range(n_c):
        weight_grad(c, dgate, 0, gg)
    for c in range(n_c):
        weight_grad(c, dup, 0, gu)

    for c in range(n_c):
        cols = slice(c * width, (c + 1) * width)
        ret_all(0, c).wait_recv()
        got = ret_recv[0, c]
        out_ref[:, cols] = (dot(wt_high, got) + dot(wt_low, got)).astype(BF16)
    for c in range(n_c):
        cols = slice(c * width, (c + 1) * width)
        ret_all(1, c).wait_recv()
        back_ref[:, cols] = dot(pick_t, ret_recv[1, c]).astype(BF16)
    for a in range(2):
        for c in range(n_c):
            a2a_all(a, c).wait_send()
            x_all(a, c).wait_send()
            red_all(a, c).wait_send()
            ret_all(a, c).wait_send()


def store_kernel(*refs):
    sem = refs[10]
    copies = [pltpu.make_async_copy(refs[i], refs[5 + i], sem.at[i]) for i in range(5)]
    for copy in copies:
        copy.start()
    for copy in copies:
        copy.wait()


def per_device(n_dp, n_e, tokens, cotangent, pick_lists, combine, w_gate, w_up, w_down):
    tok_rows, feat = tokens.shape
    capacity = pick_lists.shape[2]
    ff = w_gate.shape[1]
    slot_count = max(2, (2 * capacity + n_e - 1) // n_e)
    slot_rows = (slot_count + 15) // 16 * 16
    n_c = 4
    width = feat // n_c
    padded = n_e * slot_rows
    sent = padded - slot_rows
    total_rows = n_dp * capacity
    other_rows = total_rows - capacity
    vmem = pl.BlockSpec(memory_space=pltpu.VMEM)
    hbm = pl.BlockSpec(memory_space=pl.ANY)
    grad = jax.ShapeDtypeStruct((ff, feat), BF16)
    sems = pltpu.SemaphoreType.DMA((2, n_c))
    outs = pl.pallas_call(
        functools.partial(layer_kernel, n_dp, n_e, n_c, slot_rows),
        out_shape=(pltpu.VMEM((tok_rows, feat), BF16),) * 2 + (pltpu.VMEM((ff, feat), BF16),) * 3,
        in_specs=[pl.BlockSpec(memory_space=pltpu.HBM)] * 7,
        out_specs=(vmem,) * 5,
        scratch_shapes=[
            pltpu.VMEM((2 * n_e, capacity), jnp.int32),
            pltpu.VMEM((2 * n_e, capacity), F32),
        ]
        + [pltpu.VMEM((tok_rows, feat), BF16)] * 2
        + [pltpu.VMEM((ff, feat), BF16)] * 3
        + [
            pltpu.VMEM((2, n_c, sent, width), BF16),
            pltpu.VMEM((2, n_c, padded, width), BF16),
            pltpu.VMEM((2, n_c, total_rows, width), BF16),
            pltpu.VMEM((2, n_c, other_rows, width), BF16),
            pltpu.VMEM((2, n_c, capacity, width), BF16),
            pltpu.VMEM((2, n_c, other_rows, width), BF16),
            pltpu.VMEM((2, n_c, sent, width), BF16),
            pltpu.VMEM((2, n_c, padded, width), BF16),
            pltpu.VMEM((total_rows, ff), F32),
            pltpu.VMEM((total_rows, ff), F32),
        ]
        + [pltpu.VMEM((total_rows, ff), BF16)] * 3
        + [pltpu.SemaphoreType.DMA((9,))]
        + [sems] * 8,
        compiler_params=pltpu.CompilerParams(
            collective_id=0, has_side_effects=True, vmem_limit_bytes=59 * 2**20
        ),
        cost_estimate=pl.CostEstimate(
            flops=18 * total_rows * ff * feat,
            bytes_accessed=12 * ff * feat + 8 * tok_rows * feat,
            transcendentals=total_rows * ff,
        ),
        name="expert_layer",
    )(tokens, cotangent, pick_lists[0], combine[0], w_gate[0], w_up[0], w_down[0])
    layer_out, tokens_grad, grad_gate, grad_up, grad_down = pl.pallas_call(
        store_kernel,
        out_shape=[jax.ShapeDtypeStruct(o.shape, o.dtype) for o in outs],
        in_specs=[vmem] * 5,
        out_specs=[hbm] * 5,
        scratch_shapes=[pltpu.SemaphoreType.DMA((5,))],
        compiler_params=pltpu.CompilerParams(vmem_limit_bytes=16 * 2**20),
        name="store_results",
    )(*outs)
    return (layer_out, tokens_grad, grad_gate[None], grad_up[None], grad_down[None])


def solution(mesh):
    placed = (
        P(("dp", "expert"), None),
        P(("dp", "expert"), None),
        P("dp", None, None),
        P("dp", None, None),
        P("expert", "dp", None),
        P("expert", "dp", None),
        P("expert", "dp", None),
    )
    return jax.shard_map(
        functools.partial(per_device, mesh.shape["dp"], mesh.shape["expert"]),
        mesh=mesh,
        in_specs=placed,
        out_specs=(
            P(("dp", "expert"), None),
            P(("dp", "expert"), None),
            P("expert", "dp", None),
            P("expert", "dp", None),
            P("expert", "dp", None),
        ),
        check_vma=False,
    )
```
